32 devices in a mesh: groups: 2 (over y), col: 16 (over z, x, core).
Axes of the slice: x: 2, y: 2, z: 4, core: 2. Of those that a mesh axis runs over, the one named last changes fastest.
Arguments:
- position: float32 [3, 8192], P(None, ('groups', 'col')), parts along dimension 1, may hold values from -6 to 6
- velocity: float32 [3, 8192], P(None, ('groups', 'col')), parts along dimension 1, may hold values from -6 to 6
- old_accel: float32 [3, 8192], P(None, ('groups', 'col')), parts along dimension 1, may hold values from -6 to 6
- old_jerk: float32 [3, 8192], P(None, ('groups', 'col')), parts along dimension 1, may hold values from -6 to 6
- mass: float32 [8192], P(('groups', 'col')), parts along dimension 0, may hold values from 7.324219e-05 to 0.0007324219
- elapsed: float32 [8192], P(('groups', 'col')), parts along dimension 0, may hold values from 0.125 to 1
- active_index: int32 [8192], P(('groups', 'col')), parts along dimension 0, may hold values from 0 to 255, as said below
- active_count: int32 [32], P(('groups', 'col')), parts along dimension 0, may hold values from 1 to 256, as said below
Outputs:
- new_state: float32 [6, 8192], P(None, ('groups', 'col')), parts along dimension 1
- new_deriv: float32 [6, 8192], P(None, ('groups', 'col')), parts along dimension 1
The draws below stay inside these ranges and needn't reach their ends.
There are 2 independent parts, one for each index of `groups`. The reference program is written for one: setup_inputs(seed, part) draws one part's arguments, and reference() takes and returns one part's arrays. A program takes and returns all parts, laid end to end along the dimension named above; each array names one. Nothing has to cross between parts.
Inputs may be any that keep to these rules, and one draw needn't show every extreme that they name: `active_index`: within one device's slots all indices differ. `active_count`: some device has all 256 slots used in every draw.
All inputs are finite; a program needn't handle non-finite values.
Results may differ from the reference program's by a relative error of at most 0.00002.
Values sent between devices are 32-bit elements; how exact they have to be, the bound alone decides.
A program may use at most 64 MiB of HBM per device.

```python
import math
import jax
import jax.numpy as jnp
from jax import lax

F_DEV = 256
ACT_CAP = 256
FIELD = 4096
N_COL = 16


def draw_active_index(key, part):
    keys = jax.random.split(jax.random.fold_in(key, 11), N_COL)
    picks = jax.vmap(lambda sub: jax.random.permutation(sub, F_DEV)[:ACT_CAP])(keys)
    return picks.reshape(-1).astype(jnp.int32)


def draw_active_count(key, part):
    raw = jax.random.randint(jax.random.fold_in(key, 23), (N_COL,), 1, ACT_CAP + 1)
    counts = jnp.clip(raw * raw // ACT_CAP, 1, ACT_CAP)
    fullest = jax.random.randint(jax.random.fold_in(key, 29), (), 0, N_COL)
    counts = counts.at[fullest].set(ACT_CAP)
    return counts.astype(jnp.int32)


def steps_of(stream_key, dims, cuts, low, high):
    factor_of = 1.0
    for dim, shards_of in cuts:
        steps = jax.random.uniform(jax.random.fold_in(jax.random.fold_in(stream_key, 6), dim), (shards_of,), jnp.float32, low / len(cuts), high / len(cuts))
        factor_of = factor_of * jnp.repeat(jnp.exp(steps), dims[dim] // shards_of).reshape((-1,) + (1,) * (len(dims) - 1 - dim))
    return factor_of


def gaussian(key, extent, spread, bound, cuts=(), held_as=jnp.bfloat16):
    loudness = steps_of(key, extent, cuts, -0.22, 0.18) if cuts else 1.0
    array = jax.random.normal(key, extent, jnp.float32) * spread * loudness
    return jnp.minimum(jnp.maximum(array, -bound), bound).astype(held_as)


def setup_inputs(seed: int = 0, part: int = 0) -> dict:
    splits = jax.random.split(jax.random.key(seed), 9)
    own_keys = jax.random.split(jax.random.fold_in(splits[8], part), 9)
    position = gaussian(own_keys[0], (3, FIELD), 1.0, 6.0, ((1, 16),), jnp.float32)
    velocity = gaussian(own_keys[1], (3, FIELD), 1.0, 6.0, ((1, 16),), jnp.float32)
    old_accel = gaussian(own_keys[2], (3, FIELD), 1.0, 6.0, ((1, 16),), jnp.float32)
    old_jerk = gaussian(own_keys[3], (3, FIELD), 1.0, 6.0, ((1, 16),), jnp.float32)
    mass = jnp.clip(jnp.exp(math.log(0.0007324219) - 2.3025851 * jax.random.uniform(own_keys[4], (FIELD,), jnp.float32) ** steps_of(own_keys[4], (FIELD,), ((0, 16),), -0.2, 0.2)), 7.324219041038305e-05, 0.0007324219)
    elapsed = jnp.clip(jnp.exp(math.log(1.0) - 2.0794415 * jax.random.uniform(own_keys[5], (FIELD,), jnp.float32) ** steps_of(own_keys[5], (FIELD,), ((0, 16),), -0.2, 0.2)), 0.125, 1.0)
    active_index = draw_active_index(jax.random.fold_in(jax.random.fold_in(splits[8], part), 71), part)
    active_count = draw_active_count(jax.random.fold_in(jax.random.fold_in(splits[8], part), 71), part)
    return dict(position=position, velocity=velocity, old_accel=old_accel, old_jerk=old_jerk, mass=mass, elapsed=elapsed, active_index=active_index, active_count=active_count)


soften_sq = 0.01

def pair_terms(targets, sources):
    tgt_pos = targets[0:3]
    tgt_vel = targets[3:6]
    offset = sources[0:3][:, None, :] - tgt_pos[:, :, None]
    relvel = sources[3:6][:, None, :] - tgt_vel[:, :, None]
    dist_sq = lax.optimization_barrier(jnp.sum(offset * offset, axis=0)) + soften_sq
    inv_dist = lax.rsqrt(dist_sq)
    strength = sources[6][None, :] * inv_dist * inv_dist * inv_dist
    along = lax.optimization_barrier(jnp.sum(offset * relvel, axis=0)) / dist_sq
    new_accel = lax.optimization_barrier(jnp.sum(strength[None] * offset, axis=-1))
    new_jerk = lax.optimization_barrier(jnp.sum(strength[None] * (relvel - 3.0 * along[None] * offset), axis=-1))
    return jnp.concatenate([new_accel, new_jerk], axis=0)

def reference(position, velocity, old_accel, old_jerk, mass, elapsed, active_index, active_count):
    span = elapsed[None, :]
    pred_pos = position + span * velocity + span * span / 2.0 * old_accel + span * span * span / 6.0 * old_jerk
    pred_vel = velocity + span * old_accel + span * span / 2.0 * old_jerk
    sources = jnp.concatenate([pred_pos, pred_vel, mass[None, :]], axis=0)
    total = active_index.shape[0]
    slot_ids = jnp.arange(total, dtype=jnp.int32)
    owner = (slot_ids // ACT_CAP).astype(jnp.int32)
    global_idx = (active_index + owner * F_DEV).astype(jnp.int32)
    targets = jnp.concatenate([pred_pos[:, global_idx], pred_vel[:, global_idx]], axis=0)
    block = math.gcd(512, total)
    blocks = targets.reshape(6, total // block, block).transpose(1, 0, 2)
    derivs = lax.map(lambda tgt: pair_terms(tgt, sources), blocks)
    derivs = derivs.transpose(1, 0, 2).reshape(6, total)
    new_accel = derivs[0:3]
    new_jerk = derivs[3:6]
    step_len = elapsed[global_idx][None, :]
    x_old = position[:, global_idx]
    v_old = velocity[:, global_idx]
    a_old = old_accel[:, global_idx]
    j_old = old_jerk[:, global_idx]
    v_new = v_old + step_len / 2.0 * (a_old + new_accel) + step_len * step_len / 12.0 * (j_old - new_jerk)
    x_new = x_old + step_len / 2.0 * (v_old + v_new) + step_len * step_len / 12.0 * (a_old - new_accel)
    used = slot_ids % ACT_CAP < active_count[owner]
    state = jnp.concatenate([x_new, v_new], axis=0)
    new_state = jnp.where(used[None, :], state, jnp.zeros_like(state))
    new_deriv = jnp.where(used[None, :], derivs, jnp.zeros_like(derivs))
    return (new_state, new_deriv)
```

```python
import functools

import jax
import jax.numpy as jnp
from jax import lax
from jax.experimental import pallas as pl
from jax.experimental.pallas import tpu as pltpu
from jax.sharding import PartitionSpec as P

soften_sq = 0.01
LANES = 128
SUBLANES = 8
UNROLL = 8


def predict(x, v, a, j, t):
    pos = x + t * v + t * t / 2.0 * a + t * t * t / 6.0 * j
    vel = v + t * a + t * t / 2.0 * j
    return pos, vel


def pick(rows, index):
    width, slots = rows.shape[1], index.shape[1]
    outs = []
    for s in range(0, slots, LANES):
        idx = index[:, s : s + LANES]
        got = None
        for w in range(0, width, LANES):
            local = jnp.bitwise_and(idx, LANES - 1)
            piece = jnp.take_along_axis(
                rows[:, w : w + LANES], local, axis=1, mode="promise_in_bounds"
            )
            got = piece if got is None else jnp.where(idx >= w, piece, got)
        outs.append(got)
    return jnp.concatenate(outs, axis=1)


def kernel(
    n,
    pos_ref, vel_ref, acc_ref, jrk_ref, mass_ref, span_ref, index_ref, count_ref,
    state_ref, deriv_ref,
    field, raw, targets, total, send_sem, recv_sem,
):
    me = lax.axis_index("col")
    slots = index_ref.shape[1]
    width = mass_ref.shape[1]
    groups = slots // SUBLANES

    barrier = pltpu.get_barrier_semaphore()

    def greet(k, _):
        pl.semaphore_signal(
            barrier, inc=1, device_id={"col": lax.rem(me + k, n)},
            device_id_type=pl.DeviceIdType.MESH,
        )
        return 0

    lax.fori_loop(1, n, greet, 0)

    span = span_ref[...]
    pos, vel = predict(pos_ref[...], vel_ref[...], acc_ref[...], jrk_ref[...], span)
    field[me, 0:3] = pos
    field[me, 3:6] = vel
    field[me, 6:7] = mass_ref[...]
    field[me, 7:8] = mass_ref[...]

    pl.semaphore_wait(barrier, n - 1)

    def copy_to(k):
        peer = lax.rem(me + k, n)
        return pltpu.make_async_remote_copy(
            src_ref=field.at[me],
            dst_ref=field.at[me],
            send_sem=send_sem.at[peer],
            recv_sem=recv_sem.at[me],
            device_id={"col": peer},
            device_id_type=pl.DeviceIdType.MESH,
        )

    def send(k, _):
        copy_to(k).start()
        return 0

    lax.fori_loop(1, n, send, 0)

    raw[0:3] = pos_ref[...]
    raw[3:6] = vel_ref[...]
    raw[6:8] = jnp.zeros((2, width), jnp.float32)
    raw[8:11] = acc_ref[...]
    raw[11:14] = jrk_ref[...]
    raw[14:15] = span
    raw[15:16] = span
    index = jnp.broadcast_to(index_ref[...], (SUBLANES, slots))
    first = pick(raw[0:8], index)
    second = pick(raw[8:16], index)
    x0, v0 = first[0:3], first[3:6]
    a0, j0, dt = second[0:3], second[3:6], second[6:7]
    tpos, tvel = predict(x0, v0, a0, j0, dt)
    tcols = jnp.concatenate(
        [tpos, tvel, jnp.zeros((2, slots), jnp.float32)], axis=0
    ).T
    for c in range(6):
        targets[c] = jnp.broadcast_to(tcols[:, c : c + 1], (slots, LANES))
        total[c] = jnp.zeros((slots, LANES), jnp.float32)

    def add_block(b):
        for w in range(0, width, 2 * LANES):
            srcs = [
                [
                    jnp.broadcast_to(
                        field[b, c : c + 1, w + h : w + h + LANES], (SUBLANES, LANES)
                    )
                    for c in range(7)
                ]
                for h in range(0, min(2 * LANES, width - w), LANES)
            ]

            def add_groups(g, _):
                for u in range(UNROLL):
                    at = pl.ds(pl.multiple_of((g * UNROLL + u) * SUBLANES, SUBLANES), SUBLANES)
                    tgt = [targets[c, at] for c in range(6)]
                    sums = [total[c, at] for c in range(6)]
                    for src in srcs:
                        dx = [src[c] - tgt[c] for c in range(3)]
                        dv = [src[c + 3] - tgt[c + 3] for c in range(3)]
                        dist_sq = dx[0] * dx[0] + dx[1] * dx[1] + dx[2] * dx[2] + soften_sq
                        inv = lax.rsqrt(dist_sq)
                        inv_sq = inv * inv
                        strength = src[6] * inv * inv_sq
                        dot = dx[0] * dv[0] + dx[1] * dv[1] + dx[2] * dv[2]
                        along = 3.0 * dot * inv_sq
                        for c in range(3):
                            pull = strength * dx[c]
                            sums[c] = sums[c] + pull
                            sums[c + 3] = sums[c + 3] + (strength * dv[c] - along * pull)
                    for c in range(6):
                        total[c, at] = sums[c]
                return 0

            lax.fori_loop(0, groups // UNROLL, add_groups, 0)

    add_block(me)

    def arrive(k, _):
        b = lax.rem(me + n - k, n)
        pltpu.make_async_remote_copy(
            src_ref=field.at[b],
            dst_ref=field.at[b],
            send_sem=send_sem.at[b],
            recv_sem=recv_sem.at[b],
            device_id={"col": b},
            device_id_type=pl.DeviceIdType.MESH,
        ).wait_recv()
        add_block(b)
        return 0

    lax.fori_loop(1, n, arrive, 0)

    rows = [jnp.sum(total[c].T, axis=0, keepdims=True) for c in range(6)]
    new_acc = jnp.concatenate(rows[0:3], axis=0)
    new_jrk = jnp.concatenate(rows[3:6], axis=0)
    v1 = v0 + dt / 2.0 * (a0 + new_acc) + dt * dt / 12.0 * (j0 - new_jrk)
    x1 = x0 + dt / 2.0 * (v0 + v1) + dt * dt / 12.0 * (a0 - new_acc)
    used = lax.broadcasted_iota(jnp.int32, (3, slots), 1) < count_ref[...]
    state_ref[0:3] = jnp.where(used, x1, 0.0)
    state_ref[3:6] = jnp.where(used, v1, 0.0)
    deriv_ref[0:3] = jnp.where(used, new_acc, 0.0)
    deriv_ref[3:6] = jnp.where(used, new_jrk, 0.0)

    def sent(k, _):
        copy_to(k).wait_send()
        return 0

    lax.fori_loop(1, n, sent, 0)


def solution(mesh):
    n = mesh.shape["col"]

    def body(position, velocity, old_accel, old_jerk, mass, elapsed, active_index, active_count):
        width, slots = mass.shape[0], active_index.shape[0]
        out = jax.ShapeDtypeStruct((6, slots), jnp.float32)
        return pl.pallas_call(
            functools.partial(kernel, n),
            out_shape=(out, out),
            in_specs=[pl.BlockSpec(memory_space=pltpu.VMEM)] * 8,
            out_specs=(pl.BlockSpec(memory_space=pltpu.VMEM),) * 2,
            scratch_shapes=[
                pltpu.VMEM((n, 8, width), jnp.float32),
                pltpu.VMEM((16, width), jnp.float32),
                pltpu.VMEM((6, slots, LANES), jnp.float32),
                pltpu.VMEM((6, slots, LANES), jnp.float32),
                pltpu.SemaphoreType.DMA((n,)),
                pltpu.SemaphoreType.DMA((n,)),
            ],
            compiler_params=pltpu.CompilerParams(
                collective_id=0, has_side_effects=True, vmem_limit_bytes=16 << 20
            ),
        )(
            position, velocity, old_accel, old_jerk,
            mass[None, :], elapsed[None, :], active_index[None, :], active_count[None, :],
        )

    wide, flat = P(None, ("groups", "col")), P(("groups", "col"))
    return jax.shard_map(
        body,
        mesh=mesh,
        in_specs=(wide,) * 4 + (flat,) * 4,
        out_specs=(wide, wide),
        check_vma=False,
    )
```

```python
import functools

import jax
import jax.numpy as jnp
from jax import lax
from jax.experimental import pallas as pl
from jax.experimental.pallas import tpu as pltpu
from jax.sharding import PartitionSpec as P

soften_sq = 0.01
LANES = 128
SUBLANES = 8
UNROLL = 16


def predict(x, v, a, j, t):
    pos = x + t * v + t * t / 2.0 * a + t * t * t / 6.0 * j
    vel = v + t * a + t * t / 2.0 * j
    return pos, vel


def pick(rows, index):
    width, slots = rows.shape[1], index.shape[1]
    outs = []
    for s in range(0, slots, LANES):
        idx = index[:, s : s + LANES]
        got = None
        for w in range(0, width, LANES):
            local = jnp.bitwise_and(idx, LANES - 1)
            piece = jnp.take_along_axis(
                rows[:, w : w + LANES], local, axis=1, mode="promise_in_bounds"
            )
            got = piece if got is None else jnp.where(idx >= w, piece, got)
        outs.append(got)
    return jnp.concatenate(outs, axis=1)


def partner(me, k, n):
    if n & (n - 1):
        return lax.rem(me + k, n), lax.rem(me + n - k, n)
    other, bit = 0, 1
    while bit < n:
        other = other + lax.rem(lax.div(me, bit) + lax.div(jnp.int32(k), bit), 2) * bit
        bit *= 2
    return other, other


def each(n, step):
    if n <= 32:
        for k in range(1, n):
            step(k)
        return

    def one(k, _):
        step(k)
        return 0

    lax.fori_loop(1, n, one, 0)


def kernel(
    n,
    pos_hbm, vel_hbm, acc_hbm, jrk_hbm, mass_hbm, span_hbm, index_hbm, count_hbm,
    out_ref,
    pos_ref, vel_ref, acc_ref, jrk_ref, mass_ref, span_ref, index_ref, count_ref,
    field, raw, targets, total, send_sem, recv_sem, load_sem,
):
    me = lax.axis_index("col")
    slots = index_ref.shape[1]
    loads = [
        pltpu.make_async_copy(src, dst, load_sem.at[i])
        for i, (src, dst) in enumerate(
            (
                (pos_hbm, pos_ref), (vel_hbm, vel_ref), (acc_hbm, acc_ref),
                (jrk_hbm, jrk_ref), (span_hbm, span_ref), (mass_hbm, mass_ref),
                (index_hbm, index_ref), (count_hbm, count_ref),
            )
        )
    ]
    for load in loads:
        load.start()
    width = mass_ref.shape[1]
    groups = slots // SUBLANES

    barrier = pltpu.get_barrier_semaphore()

    def greet(k):
        pl.semaphore_signal(
            barrier, inc=1, device_id={"col": partner(me, k, n)[0]},
            device_id_type=pl.DeviceIdType.MESH,
        )

    each(n, greet)

    for load in loads:
        load.wait()

    span = span_ref[...]
    pos, vel = predict(pos_ref[...], vel_ref[...], acc_ref[...], jrk_ref[...], span)
    field[me, 0:3] = pos
    field[me, 3:6] = vel
    field[me, 6:7] = mass_ref[...]
    field[me, 7:8] = mass_ref[...]

    pl.semaphore_wait(barrier, n - 1)

    def copy_to(k):
        peer = partner(me, k, n)[0]
        return pltpu.make_async_remote_copy(
            src_ref=field.at[me],
            dst_ref=field.at[me],
            send_sem=send_sem.at[peer],
            recv_sem=recv_sem.at[me],
            device_id={"col": peer},
            device_id_type=pl.DeviceIdType.MESH,
        )

    def send(k):
        copy_to(k).start()

    each(n, send)

    raw[0:3] = pos_ref[...]
    raw[3:6] = vel_ref[...]
    raw[6:8] = jnp.zeros((2, width), jnp.float32)
    raw[8:11] = acc_ref[...]
    raw[11:14] = jrk_ref[...]
    raw[14:15] = span
    raw[15:16] = span
    index = jnp.broadcast_to(index_ref[...], (SUBLANES, slots))
    first = pick(raw[0:8], index)
    second = pick(raw[8:16], index)
    x0, v0 = first[0:3], first[3:6]
    a0, j0, dt = second[0:3], second[3:6], second[6:7]
    tpos, tvel = predict(x0, v0, a0, j0, dt)
    tcols = jnp.concatenate(
        [tpos, tvel, jnp.zeros((2, slots), jnp.float32)], axis=0
    ).T
    for c in range(6):
        targets[c] = jnp.broadcast_to(tcols[:, c : c + 1], (slots, LANES))
        total[c] = jnp.zeros((slots, LANES), jnp.float32)

    def add_block(b):
        for w in range(0, width, 2 * LANES):
            srcs = [
                [
                    jnp.broadcast_to(
                        field[b, c : c + 1, w + h : w + h + LANES], (SUBLANES, LANES)
                    )
                    for c in range(7)
                ]
                for h in range(0, min(2 * LANES, width - w), LANES)
            ]

            def add_groups(g, _):
                for u in range(UNROLL):
                    at = pl.ds(pl.multiple_of((g * UNROLL + u) * SUBLANES, SUBLANES), SUBLANES)
                    tgt = [targets[c, at] for c in range(6)]
                    sums = [total[c, at] for c in range(6)]
                    for src in srcs:
                        dx = [src[c] - tgt[c] for c in range(3)]
                        dv = [src[c + 3] - tgt[c + 3] for c in range(3)]
                        dist_sq = dx[0] * dx[0] + dx[1] * dx[1] + dx[2] * dx[2] + soften_sq
                        inv = lax.rsqrt(dist_sq)
                        inv_sq = inv * inv
                        strength = src[6] * inv * inv_sq
                        dot = dx[0] * dv[0] + dx[1] * dv[1] + dx[2] * dv[2]
                        along = 3.0 * dot * inv_sq
                        for c in range(3):
                            pull = strength * dx[c]
                            sums[c] = sums[c] + pull
                            sums[c + 3] = sums[c + 3] + (strength * dv[c] - along * pull)
                    for c in range(6):
                        total[c, at] = sums[c]
                return 0

            lax.fori_loop(0, groups // UNROLL, add_groups, 0)

    add_block(me)

    def arrive(k, _):
        b = partner(me, k, n)[1]
        pltpu.make_async_remote_copy(
            src_ref=field.at[b],
            dst_ref=field.at[b],
            send_sem=send_sem.at[b],
            recv_sem=recv_sem.at[b],
            device_id={"col": b},
            device_id_type=pl.DeviceIdType.MESH,
        ).wait_recv()
        add_block(b)
        return 0

    lax.fori_loop(1, n, arrive, 0)

    rows = [jnp.sum(total[c].T, axis=0, keepdims=True) for c in range(6)]
    new_acc = jnp.concatenate(rows[0:3], axis=0)
    new_jrk = jnp.concatenate(rows[3:6], axis=0)
    v1 = v0 + dt / 2.0 * (a0 + new_acc) + dt * dt / 12.0 * (j0 - new_jrk)
    x1 = x0 + dt / 2.0 * (v0 + v1) + dt * dt / 12.0 * (a0 - new_acc)
    used = lax.broadcasted_iota(jnp.int32, (3, slots), 1) < count_ref[0]
    out_ref[0:3] = jnp.where(used, x1, 0.0)
    out_ref[3:6] = jnp.where(used, v1, 0.0)
    out_ref[8:11] = jnp.where(used, new_acc, 0.0)
    out_ref[11:14] = jnp.where(used, new_jrk, 0.0)

    def sent(k):
        copy_to(k).wait_send()

    each(n, sent)


def solution(mesh):
    n = mesh.shape["col"]

    def body(position, velocity, old_accel, old_jerk, mass, elapsed, active_index, active_count):
        width, slots = mass.shape[0], active_index.shape[0]
        args = (
            position, velocity, old_accel, old_jerk,
            mass[None, :], elapsed[None, :], active_index[None, :], active_count,
        )
        both = pl.pallas_call(
            functools.partial(kernel, n),
            out_shape=pltpu.VMEM((16, slots), jnp.float32),
            in_specs=[pl.BlockSpec(memory_space=pltpu.HBM)] * len(args),
            out_specs=pl.BlockSpec(memory_space=pltpu.VMEM),
            scratch_shapes=[pltpu.VMEM(x.shape, x.dtype) for x in args[:-1]]
            + [pltpu.SMEM((1,), jnp.int32)]
            + [
                pltpu.VMEM((n, 8, width), jnp.float32),
                pltpu.VMEM((16, width), jnp.float32),
                pltpu.VMEM((6, slots, LANES), jnp.float32),
                pltpu.VMEM((6, slots, LANES), jnp.float32),
                pltpu.SemaphoreType.DMA((n,)),
                pltpu.SemaphoreType.DMA((n,)),
                pltpu.SemaphoreType.DMA((len(args),)),
            ],
            compiler_params=pltpu.CompilerParams(
                collective_id=0, has_side_effects=True, vmem_limit_bytes=60 << 20
            ),
            name="forces",
        )(*args)
        return both[0:6], both[8:14]

    wide, flat = P(None, ("groups", "col")), P(("groups", "col"))
    return jax.shard_map(
        body,
        mesh=mesh,
        in_specs=(wide,) * 4 + (flat,) * 4,
        out_specs=(wide, wide),
        check_vma=False,
    )
```

```python
import functools

import jax
import jax.numpy as jnp
from jax import lax
from jax.experimental import pallas as pl
from jax.experimental.pallas import tpu as pltpu
from jax.sharding import PartitionSpec as P

soften_sq = 0.01
LANES = 128
SUBLANES = 8
UNROLL = 16


def predict(x, v, a, j, t):
    pos = x + t * v + t * t / 2.0 * a + t * t * t / 6.0 * j
    vel = v + t * a + t * t / 2.0 * j
    return pos, vel


def pick(rows, index):
    width, slots = rows.shape[1], index.shape[1]
    outs = []
    for s in range(0, slots, LANES):
        idx = index[:, s : s + LANES]
        got = None
        for w in range(0, width, LANES):
            local = jnp.bitwise_and(idx, LANES - 1)
            piece = jnp.take_along_axis(
                rows[:, w : w + LANES], local, axis=1, mode="promise_in_bounds"
            )
            got = piece if got is None else jnp.where(idx >= w, piece, got)
        outs.append(got)
    return jnp.concatenate(outs, axis=1)


def xor(me, k, n):
    other, bit = 0, 1
    while bit < n:
        other = other + lax.rem(lax.div(me, bit) + lax.div(jnp.int32(k), bit), 2) * bit
        bit *= 2
    return other


def low_bit(k):
    return k & -k


def kernel(
    n,
    pos_hbm, vel_hbm, acc_hbm, jrk_hbm, mass_hbm, span_hbm, index_hbm, count_hbm,
    out_ref,
    pos_ref, vel_ref, acc_ref, jrk_ref, mass_ref, span_ref, index_ref, count_ref,
    field, raw, targets, total, send_sem, recv_sem, load_sem,
):
    me = lax.axis_index("col")
    slots = index_ref.shape[1]
    loads = [
        pltpu.make_async_copy(src, dst, load_sem.at[i])
        for i, (src, dst) in enumerate(
            (
                (pos_hbm, pos_ref), (vel_hbm, vel_ref), (acc_hbm, acc_ref),
                (jrk_hbm, jrk_ref), (span_hbm, span_ref), (mass_hbm, mass_ref),
                (index_hbm, index_ref), (count_hbm, count_ref),
            )
        )
    ]
    for load in loads:
        load.start()
    width = mass_ref.shape[1]
    groups = slots // SUBLANES

    barrier = pltpu.get_barrier_semaphore()

    bits = [1 << i for i in range(n.bit_length() - 1)]
    partners = [xor(me, bit, n) for bit in bits]
    for peer in partners:
        pl.semaphore_signal(
            barrier, inc=1, device_id={"col": peer}, device_id_type=pl.DeviceIdType.MESH
        )

    for load in loads:
        load.wait()

    span = span_ref[...]
    pos, vel = predict(pos_ref[...], vel_ref[...], acc_ref[...], jrk_ref[...], span)
    field[me, 0:3] = pos
    field[me, 3:6] = vel
    field[me, 6:7] = mass_ref[...]
    field[me, 7:8] = mass_ref[...]

    pl.semaphore_wait(barrier, len(bits))

    def hand_on(k, i):
        b = xor(me, k, n)
        return pltpu.make_async_remote_copy(
            src_ref=field.at[b],
            dst_ref=field.at[b],
            send_sem=send_sem.at[k + bits[i]],
            recv_sem=recv_sem.at[b],
            device_id={"col": partners[i]},
            device_id_type=pl.DeviceIdType.MESH,
        )

    for i in reversed(range(len(bits))):
        hand_on(0, i).start()

    raw[0:3] = pos_ref[...]
    raw[3:6] = vel_ref[...]
    raw[6:8] = jnp.zeros((2, width), jnp.float32)
    raw[8:11] = acc_ref[...]
    raw[11:14] = jrk_ref[...]
    raw[14:15] = span
    raw[15:16] = span
    index = jnp.broadcast_to(index_ref[...], (SUBLANES, slots))
    first = pick(raw[0:8], index)
    second = pick(raw[8:16], index)
    x0, v0 = first[0:3], first[3:6]
    a0, j0, dt = second[0:3], second[3:6], second[6:7]
    tpos, tvel = predict(x0, v0, a0, j0, dt)
    tcols = jnp.concatenate(
        [tpos, tvel, jnp.zeros((2, slots), jnp.float32)], axis=0
    ).T
    for c in range(6):
        targets[c] = jnp.broadcast_to(tcols[:, c : c + 1], (slots, LANES))
        total[c] = jnp.zeros((slots, LANES), jnp.float32)

    def add_block(b):
        for w in range(0, width, 2 * LANES):
            srcs = [
                [
                    jnp.broadcast_to(
                        field[b, c : c + 1, w + h : w + h + LANES], (SUBLANES, LANES)
                    )
                    for c in range(7)
                ]
                for h in range(0, min(2 * LANES, width - w), LANES)
            ]

            def add_groups(g, _):
                for u in range(UNROLL):
                    at = pl.ds(pl.multiple_of((g * UNROLL + u) * SUBLANES, SUBLANES), SUBLANES)
                    tgt = [targets[c, at] for c in range(6)]
                    sums = [total[c, at] for c in range(6)]
                    for src in srcs:
                        dx = [src[c] - tgt[c] for c in range(3)]
                        dv = [src[c + 3] - tgt[c + 3] for c in range(3)]
                        dist_sq = dx[0] * dx[0] + dx[1] * dx[1] + dx[2] * dx[2] + soften_sq
                        inv = lax.rsqrt(dist_sq)
                        inv_sq = inv * inv
                        strength = src[6] * inv * inv_sq
                        dot = dx[0] * dv[0] + dx[1] * dv[1] + dx[2] * dv[2]
                        along = 3.0 * dot * inv_sq
                        for c in range(3):
                            pull = strength * dx[c]
                            sums[c] = sums[c] + pull
                            sums[c + 3] = sums[c + 3] + (strength * dv[c] - along * pull)
                    for c in range(6):
                        total[c, at] = sums[c]
                return 0

            lax.fori_loop(0, groups // UNROLL, add_groups, 0)

    add_block(me)

    order = sorted(range(1, n), key=lambda k: (k.bit_count(), k != 1, -low_bit(k), -k))

    def arrive(step, _):
        k = sum(jnp.where(step == i, offset, 0) for i, offset in enumerate(order))
        b = xor(me, k, n)
        pltpu.make_async_remote_copy(
            src_ref=field.at[b],
            dst_ref=field.at[b],
            send_sem=send_sem.at[k],
            recv_sem=recv_sem.at[b],
            device_id={"col": partners[0]},
            device_id_type=pl.DeviceIdType.MESH,
        ).wait_recv()
        for i in reversed(range(len(bits) - 1)):

            @pl.when(lax.rem(k, 2 * bits[i]) == 0)
            def _():
                hand_on(k, i).start()

        add_block(b)
        return 0

    lax.fori_loop(0, n - 1, arrive, 0)

    rows = [jnp.sum(total[c].T, axis=0, keepdims=True) for c in range(6)]
    new_acc = jnp.concatenate(rows[0:3], axis=0)
    new_jrk = jnp.concatenate(rows[3:6], axis=0)
    v1 = v0 + dt / 2.0 * (a0 + new_acc) + dt * dt / 12.0 * (j0 - new_jrk)
    x1 = x0 + dt / 2.0 * (v0 + v1) + dt * dt / 12.0 * (a0 - new_acc)
    used = lax.broadcasted_iota(jnp.int32, (3, slots), 1) < count_ref[0]
    out_ref[0:3] = jnp.where(used, x1, 0.0)
    out_ref[3:6] = jnp.where(used, v1, 0.0)
    out_ref[8:11] = jnp.where(used, new_acc, 0.0)
    out_ref[11:14] = jnp.where(used, new_jrk, 0.0)

    for k in range(1, n):
        bit = low_bit(k)
        hand_on(k - bit, bits.index(bit)).wait_send()


def solution(mesh):
    n = mesh.shape["col"]

    def body(position, velocity, old_accel, old_jerk, mass, elapsed, active_index, active_count):
        width, slots = mass.shape[0], active_index.shape[0]
        args = (
            position, velocity, old_accel, old_jerk,
            mass[None, :], elapsed[None, :], active_index[None, :], active_count,
        )
        both = pl.pallas_call(
            functools.partial(kernel, n),
            out_shape=pltpu.VMEM((16, slots), jnp.float32),
            in_specs=[pl.BlockSpec(memory_space=pltpu.HBM)] * len(args),
            out_specs=pl.BlockSpec(memory_space=pltpu.VMEM),
            scratch_shapes=[pltpu.VMEM(x.shape, x.dtype) for x in args[:-1]]
            + [pltpu.SMEM((1,), jnp.int32)]
            + [
                pltpu.VMEM((n, 8, width), jnp.float32),
                pltpu.VMEM((16, width), jnp.float32),
                pltpu.VMEM((6, slots, LANES), jnp.float32),
                pltpu.VMEM((6, slots, LANES), jnp.float32),
                pltpu.SemaphoreType.DMA((n,)),
                pltpu.SemaphoreType.DMA((n,)),
                pltpu.SemaphoreType.DMA((len(args),)),
            ],
            compiler_params=pltpu.CompilerParams(
                collective_id=0, has_side_effects=True, vmem_limit_bytes=60 << 20
            ),
            name="forces",
        )(*args)
        return both[0:6], both[8:14]

    wide, flat = P(None, ("groups", "col")), P(("groups", "col"))
    return jax.shard_map(
        body,
        mesh=mesh,
        in_specs=(wide,) * 4 + (flat,) * 4,
        out_specs=(wide, wide),
        check_vma=False,
    )
```

```python
import functools

import jax
import jax.numpy as jnp
from jax import lax
from jax.experimental import pallas as pl
from jax.experimental.pallas import tpu as pltpu
from jax.sharding import PartitionSpec as P

soften_sq = 0.01
LANES = 128
SUBLANES = 8
UNROLL = 32


def predict(x, v, a, j, t):
    pos = x + t * v + t * t / 2.0 * a + t * t * t / 6.0 * j
    vel = v + t * a + t * t / 2.0 * j
    return pos, vel


def pick(rows, index):
    width, slots = rows.shape[1], index.shape[1]
    outs = []
    for s in range(0, slots, LANES):
        idx = index[:, s : s + LANES]
        got = None
        for w in range(0, width, LANES):
            local = jnp.bitwise_and(idx, LANES - 1)
            piece = jnp.take_along_axis(
                rows[:, w : w + LANES], local, axis=1, mode="promise_in_bounds"
            )
            got = piece if got is None else jnp.where(idx >= w, piece, got)
        outs.append(got)
    return jnp.concatenate(outs, axis=1)


def xor(me, k, n):
    other, bit = 0, 1
    while bit < n:
        other = other + lax.rem(lax.div(me, bit) + lax.div(jnp.int32(k), bit), 2) * bit
        bit *= 2
    return other


def kernel(
    n,
    pos_hbm, vel_hbm, acc_hbm, jrk_hbm, mass_hbm, span_hbm, index_hbm, count_hbm,
    out_ref,
    pos_ref, vel_ref, acc_ref, jrk_ref, mass_ref, span_ref, index_ref, count_ref,
    field, raw, targets, total, send_sem, recv_sem, load_sem,
):
    me = lax.axis_index("col")
    slots = index_ref.shape[1]
    loads = [
        pltpu.make_async_copy(src, dst, load_sem.at[i])
        for i, (src, dst) in enumerate(
            (
                (pos_hbm, pos_ref), (vel_hbm, vel_ref), (acc_hbm, acc_ref),
                (jrk_hbm, jrk_ref), (span_hbm, span_ref), (mass_hbm, mass_ref),
                (index_hbm, index_ref), (count_hbm, count_ref),
            )
        )
    ]
    for load in loads:
        load.start()
    width = mass_ref.shape[1]
    groups = slots // SUBLANES

    barrier = pltpu.get_barrier_semaphore()

    offsets = [1] + list(range(2, n, 2))
    partners = {k: xor(me, k, n) for k in offsets}
    for peer in partners.values():
        pl.semaphore_signal(
            barrier, inc=1, device_id={"col": peer}, device_id_type=pl.DeviceIdType.MESH
        )

    for load in loads:
        load.wait()

    span = span_ref[...]
    pos, vel = predict(pos_ref[...], vel_ref[...], acc_ref[...], jrk_ref[...], span)
    field[me, 0:3] = pos
    field[me, 3:6] = vel
    field[me, 6:7] = mass_ref[...]
    field[me, 7:8] = mass_ref[...]

    pl.semaphore_wait(barrier, len(offsets))

    def hand_on(k, offset):
        b = xor(me, k, n)
        return pltpu.make_async_remote_copy(
            src_ref=field.at[b],
            dst_ref=field.at[b],
            send_sem=send_sem.at[k + offset],
            recv_sem=recv_sem.at[b],
            device_id={"col": partners[offset]},
            device_id_type=pl.DeviceIdType.MESH,
        )

    for offset in offsets:
        hand_on(0, offset).start()

    raw[0:3] = pos_ref[...]
    raw[3:6] = vel_ref[...]
    raw[6:8] = jnp.zeros((2, width), jnp.float32)
    raw[8:11] = acc_ref[...]
    raw[11:14] = jrk_ref[...]
    raw[14:15] = span
    raw[15:16] = span
    index = jnp.broadcast_to(index_ref[...], (SUBLANES, slots))
    first = pick(raw[0:8], index)
    second = pick(raw[8:16], index)
    x0, v0 = first[0:3], first[3:6]
    a0, j0, dt = second[0:3], second[3:6], second[6:7]
    tpos, tvel = predict(x0, v0, a0, j0, dt)
    tcols = jnp.concatenate(
        [tpos, tvel, jnp.zeros((2, slots), jnp.float32)], axis=0
    ).T
    for c in range(6):
        targets[c] = jnp.broadcast_to(tcols[:, c : c + 1], (slots, LANES))
        total[c] = jnp.zeros((slots, LANES), jnp.float32)

    def add_block(b):
        for w in range(0, width, 2 * LANES):
            srcs = [
                [
                    jnp.broadcast_to(
                        field[b, c : c + 1, w + h : w + h + LANES], (SUBLANES, LANES)
                    )
                    for c in range(7)
                ]
                for h in range(0, min(2 * LANES, width - w), LANES)
            ]

            def add_groups(g, _):
                for u in range(UNROLL):
                    at = pl.ds(pl.multiple_of((g * UNROLL + u) * SUBLANES, SUBLANES), SUBLANES)
                    tgt = [targets[c, at] for c in range(6)]
                    sums = [total[c, at] for c in range(6)]
                    for src in srcs:
                        dx = [src[c] - tgt[c] for c in range(3)]
                        dv = [src[c + 3] - tgt[c + 3] for c in range(3)]
                        dist_sq = dx[0] * dx[0] + dx[1] * dx[1] + dx[2] * dx[2] + soften_sq
                        inv = lax.rsqrt(dist_sq)
                        inv_sq = inv * inv
                        strength = src[6] * inv * inv_sq
                        dot = dx[0] * dv[0] + dx[1] * dv[1] + dx[2] * dv[2]
                        along = 3.0 * dot * inv_sq
                        for c in range(3):
                            pull = strength * dx[c]
                            sums[c] = sums[c] + pull
                            sums[c + 3] = sums[c + 3] + (strength * dv[c] - along * pull)
                    for c in range(6):
                        total[c, at] = sums[c]
                return 0

            lax.fori_loop(0, groups // UNROLL, add_groups, 0)

    add_block(me)

    order = offsets + list(range(3, n, 2))

    def arrive(step, _):
        k = sum(jnp.where(step == i, offset, 0) for i, offset in enumerate(order))
        b = xor(me, k, n)
        pltpu.make_async_remote_copy(
            src_ref=field.at[b],
            dst_ref=field.at[b],
            send_sem=send_sem.at[k],
            recv_sem=recv_sem.at[b],
            device_id={"col": partners[1]},
            device_id_type=pl.DeviceIdType.MESH,
        ).wait_recv()

        @pl.when(lax.rem(k, 2) == 0)
        def _():
            hand_on(k, 1).start()

        add_block(b)
        return 0

    lax.fori_loop(0, n - 1, arrive, 0)

    rows = [jnp.sum(total[c].T, axis=0, keepdims=True) for c in range(6)]
    new_acc = jnp.concatenate(rows[0:3], axis=0)
    new_jrk = jnp.concatenate(rows[3:6], axis=0)
    v1 = v0 + dt / 2.0 * (a0 + new_acc) + dt * dt / 12.0 * (j0 - new_jrk)
    x1 = x0 + dt / 2.0 * (v0 + v1) + dt * dt / 12.0 * (a0 - new_acc)
    used = lax.broadcasted_iota(jnp.int32, (3, slots), 1) < count_ref[0]
    out_ref[0:3] = jnp.where(used, x1, 0.0)
    out_ref[3:6] = jnp.where(used, v1, 0.0)
    out_ref[8:11] = jnp.where(used, new_acc, 0.0)
    out_ref[11:14] = jnp.where(used, new_jrk, 0.0)

    for offset in offsets:
        hand_on(0, offset).wait_send()
    for k in range(2, n, 2):
        hand_on(k, 1).wait_send()


def solution(mesh):
    n = mesh.shape["col"]

    def body(position, velocity, old_accel, old_jerk, mass, elapsed, active_index, active_count):
        width, slots = mass.shape[0], active_index.shape[0]
        args = (
            position, velocity, old_accel, old_jerk,
            mass[None, :], elapsed[None, :], active_index[None, :], active_count,
        )
        both = pl.pallas_call(
            functools.partial(kernel, n),
            out_shape=pltpu.VMEM((16, slots), jnp.float32),
            in_specs=[pl.BlockSpec(memory_space=pltpu.HBM)] * len(args),
            out_specs=pl.BlockSpec(memory_space=pltpu.VMEM),
            scratch_shapes=[pltpu.VMEM(x.shape, x.dtype) for x in args[:-1]]
            + [pltpu.SMEM((1,), jnp.int32)]
            + [
                pltpu.VMEM((n, 8, width), jnp.float32),
                pltpu.VMEM((16, width), jnp.float32),
                pltpu.VMEM((6, slots, LANES), jnp.float32),
                pltpu.VMEM((6, slots, LANES), jnp.float32),
                pltpu.SemaphoreType.DMA((n,)),
                pltpu.SemaphoreType.DMA((n,)),
                pltpu.SemaphoreType.DMA((len(args),)),
            ],
            compiler_params=pltpu.CompilerParams(
                collective_id=0, has_side_effects=True, vmem_limit_bytes=60 << 20
            ),
            name="forces",
        )(*args)
        return both[0:6], both[8:14]

    wide, flat = P(None, ("groups", "col")), P(("groups", "col"))
    return jax.shard_map(
        body,
        mesh=mesh,
        in_specs=(wide,) * 4 + (flat,) * 4,
        out_specs=(wide, wide),
        check_vma=False,
    )
```
